32 devices in a mesh: parts: 2 (over x), frames: 16 (over z, y, core).
Axes of the slice: x: 2, y: 2, z: 4, core: 2. Of those that a mesh axis runs over, the one named last changes fastest.
Arguments:
- tokens: bfloat16 [256, 64, 1024], P(('parts', 'frames')), parts along dimension 0, may hold values from -8 to 8
- gain_frame: float32 [1024], replicated, may hold values from 0.5 to 1.5
- qkv_frame: bfloat16 [1024, 1536], replicated, may hold values from -0.4 to 0.4
- out_frame: bfloat16 [512, 1024], replicated, may hold values from -0.25 to 0.25
- gain_global: float32 [1024], replicated, may hold values from 0.5 to 1.5
- qkv_global: bfloat16 [1024, 1536], replicated, may hold values from -0.4 to 0.4
- out_global: bfloat16 [512, 1024], replicated, may hold values from -4 to 4
- covis: int32 [256, 16], P(('parts', 'frames')), parts along dimension 0, may hold values from -1 to 127, as said below
- submap_ids: int32 [256], P(('parts', 'frames')), parts along dimension 0, may hold values from 0 to 7
- submap_anchor: int32 [16], P('parts'), parts along dimension 0, may hold values from 0 to 127
Outputs:
- frame_out: bfloat16 [256, 64, 1024], P(('parts', 'frames')), parts along dimension 0
- global_update: bfloat16 [256, 64, 1024], P(('parts', 'frames')), parts along dimension 0
The draws below stay inside these ranges and needn't reach their ends.
There are 2 independent parts, one for each index of `parts`. The reference program is written for one: setup_inputs(seed, part) draws one part's arguments, and reference() takes and returns one part's arrays. A program takes and returns all parts, laid end to end along the dimension named above; an argument that names none is the same for every part. Nothing has to cross between parts.
Inputs may be any that keep to these rules, and one draw needn't show every extreme that they name: `covis`: block b holds frames b * 8 to b * 8 + 7. A frame's list holds distinct frames of other blocks, then -1 to the end. For any two different blocks d and b, exactly one frame of block d lists frames of block b, 1 to 2 of them. In every block one frame lists 16 frames.
All inputs are finite; a program needn't handle non-finite values.
Results may differ from the reference program's by a relative error of at most 0.014.
Values may be sent and summed in bfloat16 or wider, within the bound.
A program may use at most 192 MiB of HBM per device.

```python
import math
import jax
import jax.numpy as jnp
from jax import lax

D = 1024
HEADS = 8
HD = 64
P_SIZE = 64
F_DEV = 8
CAP_K = 2
NSUB = 8
INNER = 512
BLOCKS = 16
FRAMES = 128
KMAX = 16


def draw_tokens(key, part):
    key_values, key_scale = jax.random.split(jax.random.fold_in(key, 13), 2)
    values = jax.random.normal(key_values, (FRAMES, P_SIZE, D), jnp.float32)
    feature_scale = 0.3 * jnp.exp(jax.random.uniform(key_scale, (D,), jnp.float32, 0.0, math.log(10.0)))
    return jnp.clip(values * feature_scale, -8.0, 8.0).astype(jnp.bfloat16)


def projection_draw(key_seed):
    key_first = jax.random.fold_in(key_seed, 0)
    stacked = jax.random.normal(key_first, (D, 3, HEADS, HD), jnp.float32) * D ** (-0.5)
    return jnp.clip(stacked, -0.398, 0.398).reshape(D, 3 * HEADS * HD).astype(jnp.bfloat16)


def draw_qkv_frame(key, part):
    return projection_draw(jax.random.fold_in(key, 11))


def draw_qkv_global(key, part):
    return projection_draw(jax.random.fold_in(key, 12))


def draw_covis(key, part):
    seed_key = jax.random.fold_in(key, 14)
    key_order, key_frame, key_count, key_pick = jax.random.split(seed_key, 4)
    half_count = BLOCKS // 2
    block_ids = jnp.arange(BLOCKS, dtype=jnp.int32)

    def peer_positions(key_row, block):
        shuffled = jax.random.permutation(key_row, BLOCKS).astype(jnp.int32)
        ranked = jnp.where(block_ids == block, BLOCKS, shuffled)
        return jnp.argsort(jnp.argsort(ranked, stable=True), stable=True).astype(jnp.int32)
    positions = jax.vmap(peer_positions)(jax.random.split(key_order, BLOCKS), block_ids)
    frame_rank = jnp.where(positions < half_count, 0, 1 + (positions - half_count) % (F_DEV - 1)).astype(jnp.int32)
    frame_order = jax.vmap(lambda key_row: jax.random.permutation(key_row, F_DEV))(jax.random.split(key_frame, BLOCKS)).astype(jnp.int32)
    askers = jnp.take_along_axis(frame_order, frame_rank, axis=1)
    counts = jnp.where(positions < half_count, CAP_K, jax.random.randint(key_count, (BLOCKS, BLOCKS), 1, CAP_K + 1))
    counts = jnp.where(block_ids[:, None] == block_ids[None, :], 0, counts)
    picked = jax.vmap(lambda key_row: jax.random.permutation(key_row, F_DEV)[:CAP_K])(jax.random.split(key_pick, BLOCKS * BLOCKS))
    picked = picked.reshape(BLOCKS, BLOCKS, CAP_K).astype(jnp.int32)
    targets = block_ids[None, :, None] * F_DEV + picked
    living = jnp.arange(CAP_K)[None, None, :] < counts[:, :, None]

    def fill_frame(asker_row, living_row, target_row, frame_local):
        chosen = ((asker_row[:, None] == frame_local) & living_row).reshape(-1)
        slots = jnp.where(chosen, jnp.cumsum(chosen.astype(jnp.int32)) - 1, KMAX)
        return jnp.full((KMAX,), -1, jnp.int32).at[slots].set(target_row.reshape(-1), mode='drop')

    def fill_block(asker_row, living_row, target_row):
        return jax.vmap(lambda frame_local: fill_frame(asker_row, living_row, target_row, frame_local))(jnp.arange(F_DEV, dtype=jnp.int32))
    table = jax.vmap(fill_block)(askers, living, targets)
    return table.reshape(BLOCKS * F_DEV, KMAX).astype(jnp.int32)


def place_ends(result, rng, least, high):
    spot = [jax.random.randint(jax.random.fold_in(rng, axis), (), 0, length) for axis, length in enumerate(result.shape)]
    widest = result.shape.index(max(result.shape))
    next_to = spot[:widest] + [(spot[widest] + 1) % result.shape[widest]] + spot[widest + 1:]
    return result.at[tuple(spot)].set(least).at[tuple(next_to)].set(high)


def scatter_about(key, shape, deviation, bound, kind=jnp.bfloat16):
    return jnp.clip(deviation * jax.random.normal(key, shape, jnp.float32), -bound, bound).astype(kind)


def setup_inputs(seed: int = 0, part: int = 0) -> dict:
    streams_of = jax.random.split(jax.random.key(seed), 11)
    part_keys = jax.random.split(jax.random.fold_in(streams_of[10], part), 11)
    return {
        "tokens": draw_tokens(jax.random.fold_in(jax.random.fold_in(streams_of[10], part), 71), part),
        "gain_frame": jnp.clip(1.0 + 0.1 * jax.random.normal(streams_of[1], (D,), jnp.float32), 0.5, 1.5),
        "qkv_frame": draw_qkv_frame(jax.random.fold_in(streams_of[10], 71), part),
        "out_frame": scatter_about(streams_of[3], (INNER, D), INNER ** -0.5, 0.25),
        "gain_global": jnp.clip(1.0 + 0.1 * jax.random.normal(streams_of[4], (D,), jnp.float32), 0.5, 1.5),
        "qkv_global": draw_qkv_global(jax.random.fold_in(streams_of[10], 71), part),
        "out_global": scatter_about(streams_of[6], (INNER, D), (max(INNER // 256, 1)) ** -0.5, 4.0),
        "covis": draw_covis(jax.random.fold_in(jax.random.fold_in(streams_of[10], part), 71), part),
        "submap_ids": place_ends(jax.random.randint(part_keys[8], (FRAMES,), 0, NSUB), jax.random.fold_in(part_keys[8], 1), 0, NSUB - 1).astype(jnp.int32),
        "submap_anchor": place_ends(jax.random.randint(part_keys[9], (NSUB,), 0, FRAMES), jax.random.fold_in(part_keys[9], 1), 0, FRAMES - 1).astype(jnp.int32),
    }


masked_score = -1e+30

def layer_norm(values, gain_vector):
    widened = values.astype(jnp.float32)
    centre = lax.optimization_barrier(jnp.mean(widened, axis=-1, keepdims=True))
    variance = lax.optimization_barrier(jnp.mean((widened - centre) ** 2, axis=-1, keepdims=True))
    return ((widened - centre) * lax.rsqrt(variance + 1e-06) * gain_vector).astype(jnp.bfloat16)

def reference(tokens, gain_frame, qkv_frame, out_frame, gain_global, qkv_global, out_global, covis, submap_ids, submap_anchor):
    row_count = FRAMES * P_SIZE
    score_scale = HD ** (-0.5)
    normed = layer_norm(tokens.reshape(row_count, D), gain_frame)
    packed = jnp.dot(normed, qkv_frame, preferred_element_type=jnp.float32).astype(jnp.bfloat16)
    packed = packed.reshape(FRAMES, P_SIZE, 3, HEADS, HD)
    queries = packed[:, :, 0].astype(jnp.float32)
    key_rows = packed[:, :, 1].astype(jnp.float32)
    value_rows = packed[:, :, 2].astype(jnp.float32)
    scores = jnp.einsum('fqhd,fkhd->fhqk', queries, key_rows) * score_scale
    largest = lax.optimization_barrier(jnp.max(scores, axis=-1, keepdims=True))
    weights = jnp.exp(scores - largest)
    totals = lax.optimization_barrier(jnp.sum(weights, axis=-1))
    rounded = lax.optimization_barrier(weights.astype(jnp.bfloat16)).astype(jnp.float32)
    weighted_sum = jnp.einsum('fhqk,fkhd->fqhd', rounded, value_rows)
    attended = (weighted_sum / jnp.swapaxes(totals, 1, 2)[..., None]).astype(jnp.bfloat16)
    frame_out = (tokens.reshape(row_count, D).astype(jnp.float32) + jnp.dot(attended.reshape(row_count, INNER), out_frame, preferred_element_type=jnp.float32)).astype(jnp.bfloat16)
    normed_global = layer_norm(frame_out, gain_global)
    packed_global = jnp.dot(normed_global, qkv_global, preferred_element_type=jnp.float32).astype(jnp.bfloat16)
    packed_global = packed_global.reshape(FRAMES, P_SIZE, 3 * INNER)
    queries_global = packed_global[..., :INNER].reshape(FRAMES, P_SIZE, HEADS, HD)
    kv_global = packed_global[..., INNER:]
    anchor_ids = jnp.take(submap_anchor, submap_ids, axis=0).astype(jnp.int32)

    def one_frame(frame_index):
        listed = covis[frame_index]
        anchor = anchor_ids[frame_index]
        anchor_new = (anchor != frame_index) & jnp.all(listed != anchor)
        key_frames = jnp.concatenate([frame_index[None], jnp.maximum(listed, 0), anchor[None]]).astype(jnp.int32)
        visible = jnp.concatenate([jnp.ones((1,), bool), listed >= 0, anchor_new[None]])
        visible = jnp.repeat(visible, P_SIZE)
        gathered = jnp.take(kv_global, key_frames, axis=0).reshape((KMAX + 2) * P_SIZE, 2, HEADS, HD).astype(jnp.float32)
        own_queries = queries_global[frame_index].astype(jnp.float32)
        frame_scores = jnp.einsum('qhd,khd->hqk', own_queries, gathered[:, 0]) * score_scale
        frame_scores = jnp.where(visible, frame_scores, masked_score)
        frame_largest = lax.optimization_barrier(jnp.max(frame_scores, axis=-1, keepdims=True))
        frame_weights = jnp.where(visible, jnp.exp(frame_scores - frame_largest), 0.0)
        frame_totals = lax.optimization_barrier(jnp.sum(frame_weights, axis=-1))
        frame_rounded = lax.optimization_barrier(frame_weights.astype(jnp.bfloat16)).astype(jnp.float32)
        frame_sum = jnp.einsum('hqk,khd->qhd', frame_rounded, gathered[:, 1])
        return (frame_sum / frame_totals.T[..., None]).astype(jnp.bfloat16)
    attended_global = lax.map(one_frame, jnp.arange(FRAMES, dtype=jnp.int32))
    global_update = jnp.dot(attended_global.reshape(row_count, INNER), out_global, preferred_element_type=jnp.float32).astype(jnp.bfloat16)
    return (frame_out.reshape(FRAMES, P_SIZE, D), global_update.reshape(FRAMES, P_SIZE, D))
```

```python
import functools

import jax
import jax.numpy as jnp
from jax import lax
from jax.experimental import pallas as pl
from jax.experimental.pallas import tpu as pltpu
from jax.sharding import PartitionSpec as P

HEADS = 8
HD = 64
CAP_K = 2
GROUP = 4
WIDE = GROUP * HD
EXTRA = 8
ANCHOR = "butterfly"

masked_score = -1e30


def layer_norm(widened, gain_row):
    centre = jnp.mean(widened, axis=-1, keepdims=True)
    shifted = widened - centre
    variance = jnp.mean(shifted * shifted, axis=-1, keepdims=True)
    return (shifted * lax.rsqrt(variance + 1e-06) * gain_row).astype(jnp.bfloat16)


def head_masks(rows):
    head = lax.broadcasted_iota(jnp.int32, (rows, WIDE), 1) // HD
    return [head == h for h in range(GROUP)]


def attend_group(queries, keys, values, masks, visible=None):
    zero = jnp.zeros_like(queries)
    stacked = jnp.concatenate([jnp.where(m, queries, zero) for m in masks], axis=0)
    scores = lax.dot_general(
        stacked, keys, (((1,), (1,)), ((), ())), preferred_element_type=jnp.float32
    ) * HD ** (-0.5)
    if visible is not None:
        scores = jnp.where(visible, scores, masked_score)
    largest = jnp.max(scores, axis=-1, keepdims=True)
    weights = jnp.exp(scores - largest)
    if visible is not None:
        weights = jnp.where(visible, weights, 0.0)
    totals = jnp.sum(weights, axis=-1, keepdims=True)
    totals = jnp.where(totals > 0.0, totals, 1.0)
    summed = jnp.dot(weights.astype(jnp.bfloat16), values, preferred_element_type=jnp.float32)
    summed = summed * (1.0 / totals)
    rows = queries.shape[0]
    out = jnp.where(masks[0], summed[:rows], 0.0)
    for h in range(1, GROUP):
        out = jnp.where(masks[h], summed[h * rows : (h + 1) * rows], out)
    return out, largest + jnp.log(totals)


def front_kernel(
    asker,
    request,
    holding,
    held,
    tokens,
    gain_frame,
    qkv_frame,
    out_frame,
    gain_global,
    qkv_global,
    frame_out,
    packed,
    message,
    anchors,
):
    step = pl.program_id(0)
    frames, length, features = tokens.shape
    inner = HEADS * HD
    rows = frames * length
    x = tokens[...].reshape(rows, features).astype(jnp.float32)
    normed = layer_norm(x, gain_frame[...])
    first = jnp.dot(normed, qkv_frame[...], preferred_element_type=jnp.float32).astype(
        jnp.bfloat16
    )
    masks = head_masks(length)
    attended = []
    for f in range(frames):
        mine = first[f * length : (f + 1) * length]
        parts = []
        for g in range(HEADS // GROUP):
            low = g * WIDE
            out, _ = attend_group(
                mine[:, low : low + WIDE],
                mine[:, inner + low : inner + low + WIDE],
                mine[:, 2 * inner + low : 2 * inner + low + WIDE],
                masks,
            )
            parts.append(out.astype(jnp.bfloat16))
        attended.append(jnp.concatenate(parts, axis=1))
    attended = jnp.concatenate(attended, axis=0)
    after = (
        x + jnp.dot(attended, out_frame[...], preferred_element_type=jnp.float32)
    ).astype(jnp.bfloat16)
    frame_out[...] = after.reshape(frames, length, features)
    normed = layer_norm(after.astype(jnp.float32), gain_global[...])
    second = jnp.dot(normed, qkv_global[...], preferred_element_type=jnp.float32).astype(
        jnp.bfloat16
    )
    packed[pl.ds(step * frames, frames)] = second.reshape(frames, length, 3 * inner)

    @pl.when(step == pl.num_programs(0) - 1)
    def _():
        row = lax.broadcasted_iota(jnp.int32, (EXTRA, inner), 0)
        lane = lax.broadcasted_iota(jnp.int32, (EXTRA, inner), 1)

        def put(b, carry):
            message[b, :length] = packed[asker[b], :, :inner]
            note = jnp.where(lane == 0, request[2 * b], jnp.where(lane == 1, request[2 * b + 1], 0))
            note = jnp.where(row == 0, note, 0)
            message[b, length:] = note.astype(jnp.float32).astype(jnp.bfloat16)
            return carry

        lax.fori_loop(0, message.shape[0], put, 0)

        def hold(s, carry):
            taken = packed[held[s], :, inner:]
            anchors[s] = jnp.where(holding[s] > 0, taken, jnp.zeros_like(taken))
            return carry

        lax.fori_loop(0, anchors.shape[0], hold, 0)


def split_three(values):
    high = values.astype(jnp.bfloat16)
    rest = values - high.astype(jnp.float32)
    middle = rest.astype(jnp.bfloat16)
    low = (rest - middle.astype(jnp.float32)).astype(jnp.bfloat16)
    return high, middle, low


def peer_kernel(asked, received, packed, reply):
    step = pl.program_id(0)
    per_step = received.shape[0]
    length = packed.shape[1]
    inner = HEADS * HD
    masks = head_masks(length)
    rows = GROUP * length
    second_half = lax.broadcasted_iota(jnp.int32, (1, 2 * length), 1) >= length
    eye = lax.broadcasted_iota(jnp.int32, (rows, rows), 0) == lax.broadcasted_iota(
        jnp.int32, (rows, rows), 1
    )
    note_row = lax.broadcasted_iota(jnp.int32, (EXTRA, rows), 0)
    for i in range(per_step):
        b = step * per_step + i
        one, two = asked[2 * b], asked[2 * b + 1]
        visible = jnp.where(second_half, two, one) >= 0
        one, two = jnp.maximum(one, 0), jnp.maximum(two, 0)
        for g in range(HEADS // GROUP):
            low = g * WIDE
            keys = jnp.concatenate(
                [packed[f, :, inner + low : inner + low + WIDE] for f in (one, two)], axis=0
            )
            values = jnp.concatenate(
                [packed[f, :, 2 * inner + low : 2 * inner + low + WIDE] for f in (one, two)],
                axis=0,
            )
            out, lse = attend_group(
                received[i, :length, low : low + WIDE], keys, values, masks, visible
            )
            reply[i, :length, low : low + WIDE] = out.astype(jnp.bfloat16)
            line = jnp.sum(jnp.where(eye, lse, 0.0), axis=0, keepdims=True)
            high, middle, small = [p.astype(jnp.float32) for p in split_three(line)]
            note = jnp.where(
                note_row == 0,
                high,
                jnp.where(note_row == 1, middle, jnp.where(note_row == 2, small, 0.0)),
            )
            reply[i, length:, low : low + WIDE] = note.astype(jnp.bfloat16)


def own_kernel(submap, anchor_ok, packed, table, out_ref, top_ref):
    step = pl.program_id(0)
    frames, length, _ = out_ref.shape
    inner = HEADS * HD
    masks = head_masks(length)
    second_half = lax.broadcasted_iota(jnp.int32, (1, 2 * length), 1) >= length
    for i in range(frames):
        f = step * frames + i
        s = submap[f]
        visible = jnp.where(second_half, anchor_ok[f], 1) > 0
        for g in range(HEADS // GROUP):
            low = g * WIDE
            keys = jnp.concatenate(
                [packed[f, :, inner + low : inner + low + WIDE], table[s, :, low : low + WIDE]],
                axis=0,
            )
            values = jnp.concatenate(
                [
                    packed[f, :, 2 * inner + low : 2 * inner + low + WIDE],
                    table[s, :, inner + low : inner + low + WIDE],
                ],
                axis=0,
            )
            out, lse = attend_group(
                packed[f, :, low : low + WIDE], keys, values, masks, visible
            )
            out_ref[i, :, low : low + WIDE] = out
            spread = jnp.where(masks[0], lse[:length], 0.0)
            for h in range(1, GROUP):
                spread = jnp.where(masks[h], lse[h * length : (h + 1) * length], spread)
            top_ref[i, :, low : low + WIDE] = spread


def merge_kernel(asker, has_peer, replies, own_out, own_top, out_global, update, acc, top, total):
    frames, length, inner = own_out.shape
    acc[...] = own_out[...]
    top[...] = own_top[...]
    total[...] = jnp.ones_like(total)
    rows = GROUP * length
    query_of = lax.broadcasted_iota(jnp.int32, (length, rows), 1) % length
    place = query_of == lax.broadcasted_iota(jnp.int32, (length, rows), 0)
    same_head = (
        lax.broadcasted_iota(jnp.int32, (rows, WIDE), 0) // length
        == lax.broadcasted_iota(jnp.int32, (rows, WIDE), 1) // HD
    )
    spreader = jnp.where(same_head, 1.0, 0.0).astype(jnp.bfloat16)

    def add(b, carry):
        @pl.when(has_peer[b] > 0)
        def _():
            f = asker[b]
            for g in range(HEADS // GROUP):
                cols = slice(g * WIDE, (g + 1) * WIDE)
                notes = replies[b, length:, cols].astype(jnp.float32)
                stacked = jnp.concatenate(
                    [
                        jnp.where(place, notes[k : k + 1], 0.0).astype(jnp.bfloat16)
                        for k in range(3)
                    ],
                    axis=0,
                )
                spread = jnp.dot(stacked, spreader, preferred_element_type=jnp.float32)
                lse = spread[:length] + spread[length : 2 * length] + spread[2 * length :]
                before = top[f, :, cols]
                largest = jnp.maximum(before, lse)
                keep, new = jnp.exp(before - largest), jnp.exp(lse - largest)
                top[f, :, cols] = largest
                total[f, :, cols] = total[f, :, cols] * keep + new
                acc[f, :, cols] = acc[f, :, cols] * keep + (
                    replies[b, :length, cols].astype(jnp.float32) * new
                )

        return carry

    lax.fori_loop(0, replies.shape[0], add, 0)
    attended = (acc[...] / total[...]).astype(jnp.bfloat16).reshape(frames * length, inner)
    update[...] = (
        jnp.dot(attended, out_global[...], preferred_element_type=jnp.float32)
        .astype(jnp.bfloat16)
        .reshape(update.shape)
    )


def whole(shape):
    return pl.BlockSpec(shape, lambda *_: (0,) * len(shape))


def share_anchors(terms, position, block_count):
    if ANCHOR == "psum":
        return lax.psum(terms, "frames")
    shape = terms.shape
    held = terms.reshape(shape[0] * shape[1], shape[2])
    if ANCHOR == "a2a":
        pieces = held.reshape(block_count, -1, shape[2])
        got = lax.all_to_all(pieces, "frames", split_axis=0, concat_axis=0, tiled=True)
        mine = jnp.sum(got.astype(jnp.float32), axis=0).astype(jnp.bfloat16)
        return lax.all_gather(mine, "frames", tiled=True).reshape(shape)
    bits = block_count.bit_length() - 1
    for bit in range(bits):
        half = held.shape[0] // 2
        mine = (position >> bit) & 1
        keep = lax.dynamic_slice_in_dim(held, mine * half, half, 0)
        send = lax.dynamic_slice_in_dim(held, (1 - mine) * half, half, 0)
        got = lax.ppermute(send, "frames", [(d, d ^ (1 << bit)) for d in range(block_count)])
        held = keep + got
    for bit in reversed(range(bits)):
        mine = (position >> bit) & 1
        got = lax.ppermute(held, "frames", [(d, d ^ (1 << bit)) for d in range(block_count)])
        held = jnp.concatenate(
            [jnp.where(mine == 0, held, got), jnp.where(mine == 0, got, held)], axis=0
        )
    return held.reshape(shape)


def local(
    tokens,
    gain_frame,
    qkv_frame,
    out_frame,
    gain_global,
    qkv_global,
    out_global,
    covis,
    submap_ids,
    submap_anchor,
):
    frame_count, token_count, feature_count = tokens.shape
    inner_width = HEADS * HD
    block_count = lax.axis_size("frames")
    position = lax.axis_index("frames")
    submap_count = submap_anchor.shape[0]

    frame_range = jnp.arange(frame_count, dtype=jnp.int32)
    own_ids = position * frame_count + frame_range
    listed_ok = covis >= 0
    owners = jnp.where(listed_ok, covis // frame_count, -1)
    slot_index = covis % frame_count
    peer_ids = jnp.arange(block_count, dtype=jnp.int32)
    touches = owners[:, :, None] == peer_ids[None, None, :]
    asker_index = jnp.max(jnp.where(touches, frame_range[:, None, None], 0), axis=(0, 1))
    lowest = jnp.min(jnp.where(touches, slot_index[:, :, None], frame_count), axis=(0, 1))
    highest = jnp.max(jnp.where(touches, slot_index[:, :, None], -1), axis=(0, 1))
    has_peer = (highest >= 0).astype(jnp.int32)
    request = jnp.stack(
        [
            jnp.where(has_peer > 0, lowest, -1),
            jnp.where((has_peer > 0) & (highest != lowest), highest, -1),
        ],
        axis=1,
    ).reshape(-1)
    submap_range = jnp.arange(submap_count, dtype=jnp.int32)
    anchor_ids = jnp.sum(
        jnp.where(submap_ids[:, None] == submap_range, submap_anchor[None, :], 0), axis=1
    )
    in_list = jnp.any(covis == anchor_ids[:, None], axis=1)
    anchor_ok = ((anchor_ids != own_ids) & jnp.logical_not(in_list)).astype(jnp.int32)
    holding = (submap_anchor // frame_count == position).astype(jnp.int32)
    held = submap_anchor % frame_count

    rows = token_count + EXTRA
    steps = 2
    each = frame_count // steps
    frame_out, packed, message, anchor_terms = pl.pallas_call(
        front_kernel,
        grid_spec=pltpu.PrefetchScalarGridSpec(
            num_scalar_prefetch=4,
            grid=(steps,),
            in_specs=[
                pl.BlockSpec((each, token_count, feature_count), lambda i, *_: (i, 0, 0)),
                whole((1, feature_count)),
                whole(qkv_frame.shape),
                whole(out_frame.shape),
                whole((1, feature_count)),
                whole(qkv_global.shape),
            ],
            out_specs=[
                pl.BlockSpec((each, token_count, feature_count), lambda i, *_: (i, 0, 0)),
                whole((frame_count, token_count, 3 * inner_width)),
                whole((block_count, rows, inner_width)),
                whole((submap_count, token_count, 2 * inner_width)),
            ],
        ),
        out_shape=[
            jax.ShapeDtypeStruct(tokens.shape, jnp.bfloat16),
            jax.ShapeDtypeStruct((frame_count, token_count, 3 * inner_width), jnp.bfloat16),
            jax.ShapeDtypeStruct((block_count, rows, inner_width), jnp.bfloat16),
            jax.ShapeDtypeStruct((submap_count, token_count, 2 * inner_width), jnp.bfloat16),
        ],
        compiler_params=pltpu.CompilerParams(vmem_limit_bytes=52 * 2**20),
        cost_estimate=pl.CostEstimate(
            flops=4 * 10**9, bytes_accessed=15 * 10**6, transcendentals=10**6
        ),
        name="front",
    )(
        asker_index,
        request,
        holding,
        held,
        tokens,
        gain_frame.reshape(1, -1),
        qkv_frame,
        out_frame,
        gain_global.reshape(1, -1),
        qkv_global,
    )

    received = lax.all_to_all(message, "frames", split_axis=0, concat_axis=0, tiled=True)
    table = share_anchors(anchor_terms, position, block_count)

    asked = received[:, token_count, :CAP_K].astype(jnp.int32).reshape(-1)
    per_step = 4
    reply = pl.pallas_call(
        peer_kernel,
        grid_spec=pltpu.PrefetchScalarGridSpec(
            num_scalar_prefetch=1,
            grid=(block_count // per_step,),
            in_specs=[
                pl.BlockSpec((per_step, rows, inner_width), lambda i, *_: (i, 0, 0)),
                whole(packed.shape),
            ],
            out_specs=pl.BlockSpec((per_step, rows, inner_width), lambda i, *_: (i, 0, 0)),
        ),
        out_shape=jax.ShapeDtypeStruct((block_count, rows, inner_width), jnp.bfloat16),
        compiler_params=pltpu.CompilerParams(vmem_limit_bytes=24 * 2**20),
        cost_estimate=pl.CostEstimate(
            flops=2 * 10**9, bytes_accessed=4 * 10**6, transcendentals=10**6
        ),
        name="peer",
    )(asked, received, packed)

    replies = lax.all_to_all(reply, "frames", split_axis=0, concat_axis=0, tiled=True)

    own_out, own_top = pl.pallas_call(
        own_kernel,
        grid_spec=pltpu.PrefetchScalarGridSpec(
            num_scalar_prefetch=2,
            grid=(steps,),
            in_specs=[whole(packed.shape), whole(table.shape)],
            out_specs=[
                pl.BlockSpec((each, token_count, inner_width), lambda i, *_: (i, 0, 0)),
                pl.BlockSpec((each, token_count, inner_width), lambda i, *_: (i, 0, 0)),
            ],
        ),
        out_shape=[
            jax.ShapeDtypeStruct((frame_count, token_count, inner_width), jnp.float32),
            jax.ShapeDtypeStruct((frame_count, token_count, inner_width), jnp.float32),
        ],
        compiler_params=pltpu.CompilerParams(vmem_limit_bytes=24 * 2**20),
        cost_estimate=pl.CostEstimate(
            flops=10**9, bytes_accessed=4 * 10**6, transcendentals=10**6
        ),
        name="own",
    )(submap_ids, anchor_ok, packed, table)

    global_update = pl.pallas_call(
        merge_kernel,
        grid_spec=pltpu.PrefetchScalarGridSpec(
            num_scalar_prefetch=2,
            grid=(1,),
            in_specs=[
                whole(replies.shape),
                whole(own_out.shape),
                whole(own_top.shape),
                whole(out_global.shape),
            ],
            out_specs=whole(tokens.shape),
            scratch_shapes=[pltpu.VMEM(own_out.shape, jnp.float32)] * 3,
        ),
        out_shape=jax.ShapeDtypeStruct(tokens.shape, jnp.bfloat16),
        compiler_params=pltpu.CompilerParams(vmem_limit_bytes=40 * 2**20),
        cost_estimate=pl.CostEstimate(
            flops=10**9, bytes_accessed=6 * 10**6, transcendentals=10**6
        ),
        name="merge",
    )(asker_index, has_peer, replies, own_out, own_top, out_global)
    return frame_out, global_update


def solution(mesh):
    return jax.shard_map(
        local,
        mesh=mesh,
        in_specs=(
            P(("parts", "frames"), None, None),
            P(),
            P(),
            P(),
            P(),
            P(),
            P(),
            P(("parts", "frames"), None),
            P(("parts", "frames")),
            P("parts"),
        ),
        out_specs=(P(("parts", "frames"), None, None), P(("parts", "frames"), None, None)),
        check_vma=False,
    )
```

```python
import functools

import jax
import jax.numpy as jnp
from jax import lax
from jax.experimental import pallas as pl
from jax.experimental.pallas import tpu as pltpu
from jax.sharding import PartitionSpec as P

HEADS = 8
HD = 64
CAP_K = 2
GROUP = 4
WIDE = GROUP * HD
PIECE = 16
MESH = pl.DeviceIdType.MESH

masked_score = -1e30


def layer_norm(widened, gain_row):
    centre = jnp.mean(widened, axis=-1, keepdims=True)
    shifted = widened - centre
    variance = jnp.mean(shifted * shifted, axis=-1, keepdims=True)
    return (shifted * lax.rsqrt(variance + 1e-06) * gain_row).astype(jnp.bfloat16)


def head_masks(rows):
    head = lax.broadcasted_iota(jnp.int32, (rows, WIDE), 1) // HD
    return [head == h for h in range(GROUP)]


def attend_group(queries, keys, values, masks, visible=None):
    zero = jnp.zeros_like(queries)
    stacked = jnp.concatenate([jnp.where(m, queries, zero) for m in masks], axis=0)
    scores = lax.dot_general(
        stacked, keys, (((1,), (1,)), ((), ())), preferred_element_type=jnp.float32
    ) * HD ** (-0.5)
    if visible is not None:
        scores = jnp.where(visible, scores, masked_score)
    largest = jnp.max(scores, axis=-1, keepdims=True)
    weights = jnp.exp(scores - largest)
    if visible is not None:
        weights = jnp.where(visible, weights, 0.0)
    totals = jnp.sum(weights, axis=-1, keepdims=True)
    totals = jnp.where(totals > 0.0, totals, 1.0)
    summed = jnp.dot(weights.astype(jnp.bfloat16), values, preferred_element_type=jnp.float32)
    summed = summed * (1.0 / totals)
    rows = queries.shape[0]
    out = jnp.where(masks[0], summed[:rows], 0.0)
    for h in range(1, GROUP):
        out = jnp.where(masks[h], summed[h * rows : (h + 1) * rows], out)
    return out, largest + jnp.log(totals)


def front_kernel(
    asker,
    request,
    holding,
    held,
    tokens,
    gain_frame,
    qkv_frame,
    out_frame,
    gain_global,
    qkv_global,
    frame_out,
    packed,
    message,
    notes,
    anchors,
):
    step = pl.program_id(0)
    frames, length, features = tokens.shape
    inner = HEADS * HD
    rows = frames * length
    x = tokens[...].reshape(rows, features).astype(jnp.float32)
    normed = layer_norm(x, gain_frame[...])
    first = jnp.dot(normed, qkv_frame[...], preferred_element_type=jnp.float32).astype(
        jnp.bfloat16
    )
    masks = head_masks(length)
    attended = []
    for f in range(frames):
        mine = first[f * length : (f + 1) * length]
        parts = []
        for g in range(HEADS // GROUP):
            low = g * WIDE
            out, _ = attend_group(
                mine[:, low : low + WIDE],
                mine[:, inner + low : inner + low + WIDE],
                mine[:, 2 * inner + low : 2 * inner + low + WIDE],
                masks,
            )
            parts.append(out.astype(jnp.bfloat16))
        attended.append(jnp.concatenate(parts, axis=1))
    attended = jnp.concatenate(attended, axis=0)
    after = (
        x + jnp.dot(attended, out_frame[...], preferred_element_type=jnp.float32)
    ).astype(jnp.bfloat16)
    frame_out[...] = after.reshape(frames, length, features)
    normed = layer_norm(after.astype(jnp.float32), gain_global[...])
    second = jnp.dot(normed, qkv_global[...], preferred_element_type=jnp.float32).astype(
        jnp.bfloat16
    )
    packed[pl.ds(step * frames, frames)] = second.reshape(frames, length, 3 * inner)

    @pl.when(step == pl.num_programs(0) - 1)
    def _():
        row = lax.broadcasted_iota(jnp.int32, notes.shape[1:], 0)
        lane = lax.broadcasted_iota(jnp.int32, notes.shape[1:], 1)
        frame_of_key = (row * lane.shape[1] + lane) // length

        def put(b, carry):
            message[b] = packed[asker[b], :, :inner]
            wanted = (frame_of_key == request[2 * b]) | (frame_of_key == request[2 * b + 1])
            notes[b] = jnp.where(wanted, 1.0, 0.0)
            return carry

        lax.fori_loop(0, message.shape[0], put, 0)
        count = length // PIECE

        def hold(s, carry):
            taken = packed[held[s], :, inner:]
            taken = jnp.where(holding[s] > 0, taken, jnp.zeros_like(taken))
            for r in range(count):
                for c in range(2):
                    anchors[(s * count + r) * 2 + c] = taken[
                        r * PIECE : (r + 1) * PIECE, c * inner : (c + 1) * inner
                    ]
            return carry

        lax.fori_loop(0, held.shape[0], hold, 0)


def split_three(values):
    high = values.astype(jnp.bfloat16)
    rest = values - high.astype(jnp.float32)
    middle = rest.astype(jnp.bfloat16)
    low = (rest - middle.astype(jnp.float32)).astype(jnp.bfloat16)
    return high, middle, low


def exchange_kernel(
    n,
    queries,
    notes,
    packed,
    anchors,
    replies,
    stats,
    table,
    queries_in,
    notes_in,
    reply,
    stat,
    arrived,
    work,
    query_sent,
    query_got,
    note_sent,
    note_got,
    reply_sent,
    reply_got,
    stat_sent,
    stat_got,
    anchor_sent,
    anchor_got,
):
    me = lax.axis_index("frames")
    frames, length, _ = packed.shape
    inner = HEADS * HD
    keys_in_all = frames * length

    def copy(source, target, sent, got, device):
        return pltpu.make_async_remote_copy(
            src_ref=source,
            dst_ref=target,
            send_sem=sent,
            recv_sem=got,
            device_id={"frames": device},
            device_id_type=MESH,
        )

    def query_copies(k):
        peer = lax.rem(me + k, n)
        return (
            copy(queries.at[peer], queries_in.at[me], query_sent.at[k], query_got.at[k], peer),
            copy(notes.at[peer], notes_in.at[me], note_sent.at[k], note_got.at[k], peer),
        )

    def reply_copies(k):
        peer = lax.rem(me - k + n, n)
        return (
            copy(reply.at[k], replies.at[me], reply_sent.at[k], reply_got.at[k], peer),
            copy(stat.at[k], stats.at[me], stat_sent.at[k], stat_got.at[k], peer),
        )

    barrier = pltpu.get_barrier_semaphore()

    def greet(k, carry):
        pl.semaphore_signal(
            barrier, inc=1, device_id={"frames": lax.rem(me + k, n)}, device_id_type=MESH
        )
        return carry

    lax.fori_loop(1, n, greet, 0)
    work[...] = anchors[...]
    replies[me] = jnp.zeros(replies.shape[1:], replies.dtype)
    stats[me] = jnp.zeros(stats.shape[1:], stats.dtype)
    pl.semaphore_wait(barrier, n - 1)

    stages = n.bit_length() - 1
    pieces = table.shape[0]

    def ask(k, carry):
        for c in query_copies(k):
            c.start()
        return carry

    base = me * 0
    size = pieces
    bounds = [1 + (n - 1) * i // stages for i in range(stages + 1)]
    for i in range(stages):
        half = size // 2
        bit = (me // 2**i) % 2
        partner = me + 2**i * (1 - 2 * bit)
        mine = base + bit * half
        other = base + (1 - bit) * half
        start = pieces - size
        moving = copy(
            work.at[pl.ds(other, half)],
            arrived.at[pl.ds(start, half)],
            anchor_sent.at[i],
            anchor_got.at[i],
            partner,
        )
        moving.start()
        lax.fori_loop(bounds[i], bounds[i + 1], ask, 0)
        moving.wait()
        work[pl.ds(mine, half)] = work[pl.ds(mine, half)] + arrived[pl.ds(start, half)]
        base, size = mine, half
    table[pl.ds(base, size)] = work[pl.ds(base, size)]

    masks = head_masks(length)
    rows = GROUP * length
    eye = lax.broadcasted_iota(jnp.int32, (rows, rows), 0) == lax.broadcasted_iota(
        jnp.int32, (rows, rows), 1
    )

    def answer(k, carry):
        source = lax.rem(me - k + n, n)
        for c in query_copies(k):
            c.wait_recv()
        note = notes_in[source]
        lines = keys_in_all // note.shape[1]
        visible = jnp.concatenate([note[j : j + 1] for j in range(lines)], axis=1) > 0.5
        pieces_out = []
        for g in range(HEADS // GROUP):
            low = g * WIDE
            keys = packed[:, :, inner + low : inner + low + WIDE].reshape(keys_in_all, WIDE)
            values = packed[:, :, 2 * inner + low : 2 * inner + low + WIDE].reshape(
                keys_in_all, WIDE
            )
            out, lse = attend_group(
                queries_in[source, :, low : low + WIDE], keys, values, masks, visible
            )
            reply[k, :, low : low + WIDE] = out.astype(jnp.bfloat16)
            line = jnp.sum(jnp.where(eye, lse, 0.0), axis=0, keepdims=True)
            width = note.shape[1]
            pieces_out += [line[:, j * width : (j + 1) * width] for j in range(rows // width)]
        spare = jnp.zeros((note.shape[0] - len(pieces_out), note.shape[1]), jnp.float32)
        stat[k] = jnp.concatenate(pieces_out + [spare], axis=0)
        for c in reply_copies(k):
            c.start()
        return carry

    for i in reversed(range(stages)):
        bit = (me // 2**i) % 2
        partner = me + 2**i * (1 - 2 * bit)
        moving = copy(
            table.at[pl.ds(base, size)],
            table.at[pl.ds(base, size)],
            anchor_sent.at[stages + i],
            anchor_got.at[stages + i],
            partner,
        )
        moving.start()
        lax.fori_loop(bounds[stages - 1 - i], bounds[stages - i], answer, 0)
        moving.wait()
        base, size = base - bit * size, 2 * size

    def finish(k, carry):
        for c in query_copies(k):
            c.wait_send()
        for c in reply_copies(k):
            c.wait()
        return carry

    lax.fori_loop(1, n, finish, 0)


def own_kernel(submap, anchor_ok, packed, table, out_ref, top_ref):
    step = pl.program_id(0)
    frames, length, _ = out_ref.shape
    inner = HEADS * HD
    masks = head_masks(length)
    second_half = lax.broadcasted_iota(jnp.int32, (1, 2 * length), 1) >= length
    for i in range(frames):
        f = step * frames + i
        s = submap[f]
        visible = jnp.where(second_half, anchor_ok[f], 1) > 0
        for g in range(HEADS // GROUP):
            low = g * WIDE
            keys = jnp.concatenate(
                [packed[f, :, inner + low : inner + low + WIDE], table[s, :, 0, :, low : low + WIDE].reshape(length, WIDE)],
                axis=0,
            )
            values = jnp.concatenate(
                [
                    packed[f, :, 2 * inner + low : 2 * inner + low + WIDE],
                    table[s, :, 1, :, low : low + WIDE].reshape(length, WIDE),
                ],
                axis=0,
            )
            out, lse = attend_group(
                packed[f, :, low : low + WIDE], keys, values, masks, visible
            )
            out_ref[i, :, low : low + WIDE] = out
            spread = jnp.where(masks[0], lse[:length], 0.0)
            for h in range(1, GROUP):
                spread = jnp.where(masks[h], lse[h * length : (h + 1) * length], spread)
            top_ref[i, :, low : low + WIDE] = spread


def merge_kernel(asker, has_peer, replies, stats, own_out, own_top, out_global, update, acc, top, total):
    frames, length, inner = own_out.shape
    acc[...] = own_out[...]
    top[...] = own_top[...]
    total[...] = jnp.ones_like(total)
    rows = GROUP * length
    query_of = lax.broadcasted_iota(jnp.int32, (length, rows), 1) % length
    place = query_of == lax.broadcasted_iota(jnp.int32, (length, rows), 0)
    same_head = (
        lax.broadcasted_iota(jnp.int32, (rows, WIDE), 0) // length
        == lax.broadcasted_iota(jnp.int32, (rows, WIDE), 1) // HD
    )
    spreader = jnp.where(same_head, 1.0, 0.0).astype(jnp.bfloat16)

    def add(b, carry):
        @pl.when(has_peer[b] > 0)
        def _():
            f = asker[b]
            for g in range(HEADS // GROUP):
                cols = slice(g * WIDE, (g + 1) * WIDE)
                lines = stats[b]
                count = rows // lines.shape[1]
                line = jnp.concatenate(
                    [lines[j : j + 1] for j in range(g * count, (g + 1) * count)], axis=1
                )
                notes = split_three(line)
                stacked = jnp.concatenate(
                    [
                        jnp.where(place, part.astype(jnp.float32), 0.0).astype(jnp.bfloat16)
                        for part in notes
                    ],
                    axis=0,
                )
                spread = jnp.dot(stacked, spreader, preferred_element_type=jnp.float32)
                lse = spread[:length] + spread[length : 2 * length] + spread[2 * length :]
                before = top[f, :, cols]
                largest = jnp.maximum(before, lse)
                keep, new = jnp.exp(before - largest), jnp.exp(lse - largest)
                top[f, :, cols] = largest
                total[f, :, cols] = total[f, :, cols] * keep + new
                acc[f, :, cols] = acc[f, :, cols] * keep + (
                    replies[b, :, cols].astype(jnp.float32) * new
                )

        return carry

    lax.fori_loop(0, replies.shape[0], add, 0)
    attended = (acc[...] / total[...]).astype(jnp.bfloat16).reshape(frames * length, inner)
    update[...] = (
        jnp.dot(attended, out_global[...], preferred_element_type=jnp.float32)
        .astype(jnp.bfloat16)
        .reshape(update.shape)
    )


def whole(shape):
    return pl.BlockSpec(shape, lambda *_: (0,) * len(shape))


def local(
    tokens,
    gain_frame,
    qkv_frame,
    out_frame,
    gain_global,
    qkv_global,
    out_global,
    covis,
    submap_ids,
    submap_anchor,
):
    frame_count, token_count, feature_count = tokens.shape
    inner_width = HEADS * HD
    block_count = lax.axis_size("frames")
    position = lax.axis_index("frames")
    submap_count = submap_anchor.shape[0]

    frame_range = jnp.arange(frame_count, dtype=jnp.int32)
    own_ids = position * frame_count + frame_range
    listed_ok = covis >= 0
    owners = jnp.where(listed_ok, covis // frame_count, -1)
    slot_index = covis % frame_count
    peer_ids = jnp.arange(block_count, dtype=jnp.int32)
    touches = owners[:, :, None] == peer_ids[None, None, :]
    asker_index = jnp.max(jnp.where(touches, frame_range[:, None, None], 0), axis=(0, 1))
    lowest = jnp.min(jnp.where(touches, slot_index[:, :, None], frame_count), axis=(0, 1))
    highest = jnp.max(jnp.where(touches, slot_index[:, :, None], -1), axis=(0, 1))
    has_peer = (highest >= 0).astype(jnp.int32)
    request = jnp.stack(
        [
            jnp.where(has_peer > 0, lowest, -1),
            jnp.where((has_peer > 0) & (highest != lowest), highest, -1),
        ],
        axis=1,
    ).reshape(-1)
    submap_range = jnp.arange(submap_count, dtype=jnp.int32)
    anchor_ids = jnp.sum(
        jnp.where(submap_ids[:, None] == submap_range, submap_anchor[None, :], 0), axis=1
    )
    in_list = jnp.any(covis == anchor_ids[:, None], axis=1)
    anchor_ok = ((anchor_ids != own_ids) & jnp.logical_not(in_list)).astype(jnp.int32)
    holding = (submap_anchor // frame_count == position).astype(jnp.int32)
    held = submap_anchor % frame_count

    note_shape = (block_count, 8, 128)
    piece_count = submap_count * token_count // PIECE * 2
    pieces = (piece_count, PIECE, inner_width)
    assert frame_count * token_count <= 1024 and piece_count % block_count == 0
    steps = 2
    each = frame_count // steps
    frame_out, packed, message, notes, anchor_terms = pl.pallas_call(
        front_kernel,
        grid_spec=pltpu.PrefetchScalarGridSpec(
            num_scalar_prefetch=4,
            grid=(steps,),
            in_specs=[
                pl.BlockSpec((each, token_count, feature_count), lambda i, *_: (i, 0, 0)),
                whole((1, feature_count)),
                whole(qkv_frame.shape),
                whole(out_frame.shape),
                whole((1, feature_count)),
                whole(qkv_global.shape),
            ],
            out_specs=[
                pl.BlockSpec((each, token_count, feature_count), lambda i, *_: (i, 0, 0)),
                whole((frame_count, token_count, 3 * inner_width)),
                whole((block_count, token_count, inner_width)),
                whole(note_shape),
                whole(pieces),
            ],
        ),
        out_shape=[
            jax.ShapeDtypeStruct(tokens.shape, jnp.bfloat16),
            jax.ShapeDtypeStruct((frame_count, token_count, 3 * inner_width), jnp.bfloat16),
            jax.ShapeDtypeStruct((block_count, token_count, inner_width), jnp.bfloat16),
            jax.ShapeDtypeStruct(note_shape, jnp.float32),
            jax.ShapeDtypeStruct(pieces, jnp.bfloat16),
        ],
        compiler_params=pltpu.CompilerParams(vmem_limit_bytes=52 * 2**20),
        cost_estimate=pl.CostEstimate(
            flops=4 * 10**9, bytes_accessed=15 * 10**6, transcendentals=10**6
        ),
        name="front",
    )(
        asker_index,
        request,
        holding,
        held,
        tokens,
        gain_frame.reshape(1, -1),
        qkv_frame,
        out_frame,
        gain_global.reshape(1, -1),
        qkv_global,
    )

    stages = block_count.bit_length() - 1
    in_vmem = pl.BlockSpec(memory_space=pltpu.VMEM)
    per_peer = pltpu.SemaphoreType.DMA((block_count,))
    replies, stats, table = pl.pallas_call(
        functools.partial(exchange_kernel, block_count),
        in_specs=[in_vmem] * 4,
        out_specs=[in_vmem] * 3,
        out_shape=[
            jax.ShapeDtypeStruct(message.shape, jnp.bfloat16),
            jax.ShapeDtypeStruct(note_shape, jnp.float32),
            jax.ShapeDtypeStruct(pieces, jnp.bfloat16),
        ],
        scratch_shapes=[
            pltpu.VMEM(message.shape, jnp.bfloat16),
            pltpu.VMEM(note_shape, jnp.float32),
            pltpu.VMEM(message.shape, jnp.bfloat16),
            pltpu.VMEM(note_shape, jnp.float32),
            pltpu.VMEM(pieces, jnp.bfloat16),
            pltpu.VMEM(pieces, jnp.bfloat16),
        ]
        + [per_peer] * 8
        + [pltpu.SemaphoreType.DMA((2 * stages,))] * 2,
        compiler_params=pltpu.CompilerParams(
            collective_id=0, has_side_effects=True, vmem_limit_bytes=44 * 2**20
        ),
        cost_estimate=pl.CostEstimate(
            flops=4 * 10**9, bytes_accessed=8 * 10**6, transcendentals=4 * 10**6
        ),
        name="exchange",
    )(message, notes, packed, anchor_terms)
    table = table.reshape(submap_count, token_count // PIECE, 2, PIECE, inner_width)

    own_out, own_top = pl.pallas_call(
        own_kernel,
        grid_spec=pltpu.PrefetchScalarGridSpec(
            num_scalar_prefetch=2,
            grid=(steps,),
            in_specs=[whole(packed.shape), whole(table.shape)],
            out_specs=[
                pl.BlockSpec((each, token_count, inner_width), lambda i, *_: (i, 0, 0)),
                pl.BlockSpec((each, token_count, inner_width), lambda i, *_: (i, 0, 0)),
            ],
        ),
        out_shape=[
            jax.ShapeDtypeStruct((frame_count, token_count, inner_width), jnp.float32),
            jax.ShapeDtypeStruct((frame_count, token_count, inner_width), jnp.float32),
        ],
        compiler_params=pltpu.CompilerParams(vmem_limit_bytes=24 * 2**20),
        cost_estimate=pl.CostEstimate(
            flops=10**9, bytes_accessed=4 * 10**6, transcendentals=10**6
        ),
        name="own",
    )(submap_ids, anchor_ok, packed, table)

    global_update = pl.pallas_call(
        merge_kernel,
        grid_spec=pltpu.PrefetchScalarGridSpec(
            num_scalar_prefetch=2,
            grid=(1,),
            in_specs=[
                whole(replies.shape),
                whole(stats.shape),
                whole(own_out.shape),
                whole(own_top.shape),
                whole(out_global.shape),
            ],
            out_specs=whole(tokens.shape),
            scratch_shapes=[pltpu.VMEM(own_out.shape, jnp.float32)] * 3,
        ),
        out_shape=jax.ShapeDtypeStruct(tokens.shape, jnp.bfloat16),
        compiler_params=pltpu.CompilerParams(vmem_limit_bytes=40 * 2**20),
        cost_estimate=pl.CostEstimate(
            flops=10**9, bytes_accessed=6 * 10**6, transcendentals=10**6
        ),
        name="merge",
    )(asker_index, has_peer, replies, stats, own_out, own_top, out_global)
    return frame_out, global_update


def solution(mesh):
    return jax.shard_map(
        local,
        mesh=mesh,
        in_specs=(
            P(("parts", "frames"), None, None),
            P(),
            P(),
            P(),
            P(),
            P(),
            P(),
            P(("parts", "frames"), None),
            P(("parts", "frames")),
            P("parts"),
        ),
        out_specs=(P(("parts", "frames"), None, None), P(("parts", "frames"), None, None)),
        check_vma=False,
    )
```

```python
import functools

import jax
import jax.numpy as jnp
from jax import lax
from jax.experimental import pallas as pl
from jax.experimental.pallas import tpu as pltpu
from jax.sharding import PartitionSpec as P

HEADS = 8
HD = 64
CAP_K = 2
GROUP = 4
WIDE = GROUP * HD
PIECE = 16
MESH = pl.DeviceIdType.MESH

masked_score = -1e30


def layer_norm(widened, gain_row):
    centre = jnp.mean(widened, axis=-1, keepdims=True)
    shifted = widened - centre
    variance = jnp.mean(shifted * shifted, axis=-1, keepdims=True)
    return (shifted * lax.rsqrt(variance + 1e-06) * gain_row).astype(jnp.bfloat16)


def head_masks(rows):
    head = lax.broadcasted_iota(jnp.int32, (rows, WIDE), 1) // HD
    return [head == h for h in range(GROUP)]


def attend_group(queries, keys, values, masks, visible=None):
    zero = jnp.zeros_like(queries)
    stacked = jnp.concatenate([jnp.where(m, queries, zero) for m in masks], axis=0)
    scores = lax.dot_general(
        stacked, keys, (((1,), (1,)), ((), ())), preferred_element_type=jnp.float32
    ) * HD ** (-0.5)
    if visible is not None:
        scores = jnp.where(visible, scores, masked_score)
    largest = jnp.max(scores, axis=-1, keepdims=True)
    weights = jnp.exp(scores - largest)
    if visible is not None:
        weights = jnp.where(visible, weights, 0.0)
    totals = jnp.sum(weights, axis=-1, keepdims=True)
    totals = jnp.where(totals > 0.0, totals, 1.0)
    summed = jnp.dot(weights.astype(jnp.bfloat16), values, preferred_element_type=jnp.float32)
    summed = summed * (1.0 / totals)
    rows = queries.shape[0]
    out = jnp.where(masks[0], summed[:rows], 0.0)
    for h in range(1, GROUP):
        out = jnp.where(masks[h], summed[h * rows : (h + 1) * rows], out)
    return out, largest + jnp.log(totals)


def front_kernel(
    asker,
    request,
    holding,
    held,
    tokens,
    gain_frame,
    qkv_frame,
    out_frame,
    gain_global,
    qkv_global,
    frame_out,
    packed,
    message,
    notes,
    anchors,
):
    step = pl.program_id(0)
    frames, length, features = tokens.shape
    inner = HEADS * HD
    rows = frames * length
    x = tokens[...].reshape(rows, features).astype(jnp.float32)
    normed = layer_norm(x, gain_frame[...])
    first = jnp.dot(normed, qkv_frame[...], preferred_element_type=jnp.float32).astype(
        jnp.bfloat16
    )
    masks = head_masks(length)
    attended = []
    for f in range(frames):
        mine = first[f * length : (f + 1) * length]
        parts = []
        for g in range(HEADS // GROUP):
            low = g * WIDE
            out, _ = attend_group(
                mine[:, low : low + WIDE],
                mine[:, inner + low : inner + low + WIDE],
                mine[:, 2 * inner + low : 2 * inner + low + WIDE],
                masks,
            )
            parts.append(out.astype(jnp.bfloat16))
        attended.append(jnp.concatenate(parts, axis=1))
    attended = jnp.concatenate(attended, axis=0)
    after = (
        x + jnp.dot(attended, out_frame[...], preferred_element_type=jnp.float32)
    ).astype(jnp.bfloat16)
    frame_out[...] = after.reshape(frames, length, features)
    normed = layer_norm(after.astype(jnp.float32), gain_global[...])
    second = jnp.dot(normed, qkv_global[...], preferred_element_type=jnp.float32).astype(
        jnp.bfloat16
    )
    packed[pl.ds(step * frames, frames)] = second.reshape(frames, length, 3 * inner)

    @pl.when(step == pl.num_programs(0) - 1)
    def _():
        row = lax.broadcasted_iota(jnp.int32, notes.shape[1:], 0)
        lane = lax.broadcasted_iota(jnp.int32, notes.shape[1:], 1)
        frame_of_key = (row * lane.shape[1] + lane) // length

        def put(b, carry):
            message[b] = packed[asker[b], :, :inner]
            wanted = (frame_of_key == request[2 * b]) | (frame_of_key == request[2 * b + 1])
            notes[b] = jnp.where(wanted, 1.0, 0.0)
            return carry

        lax.fori_loop(0, message.shape[0], put, 0)
        count = length // PIECE

        def hold(s, carry):
            taken = packed[held[s], :, inner:]
            taken = jnp.where(holding[s] > 0, taken, jnp.zeros_like(taken))
            for r in range(count):
                for c in range(2):
                    anchors[(s * count + r) * 2 + c] = taken[
                        r * PIECE : (r + 1) * PIECE, c * inner : (c + 1) * inner
                    ]
            return carry

        lax.fori_loop(0, held.shape[0], hold, 0)


def split_three(values):
    high = values.astype(jnp.bfloat16)
    rest = values - high.astype(jnp.float32)
    middle = rest.astype(jnp.bfloat16)
    low = (rest - middle.astype(jnp.float32)).astype(jnp.bfloat16)
    return high, middle, low


def exchange_kernel(
    n,
    queries,
    notes,
    packed,
    anchors,
    replies,
    stats,
    table,
    queries_in,
    notes_in,
    reply,
    stat,
    arrived,
    work,
    query_sent,
    query_got,
    note_sent,
    note_got,
    reply_sent,
    reply_got,
    stat_sent,
    stat_got,
    anchor_sent,
    anchor_got,
):
    me = lax.axis_index("frames")
    frames, length, _ = packed.shape
    inner = HEADS * HD
    keys_in_all = frames * length

    def copy(source, target, sent, got, device):
        return pltpu.make_async_remote_copy(
            src_ref=source,
            dst_ref=target,
            send_sem=sent,
            recv_sem=got,
            device_id={"frames": device},
            device_id_type=MESH,
        )

    def offset(j):
        odd = (j - 1) % 2
        return n // 2 + (1 - odd) * ((j - 1) // 2) - odd * (j // 2)

    def query_copies(k):
        peer = lax.rem(me + offset(k), n)
        return (
            copy(queries.at[peer], queries_in.at[me], query_sent.at[k], query_got.at[k], peer),
            copy(notes.at[peer], notes_in.at[me], note_sent.at[k], note_got.at[k], peer),
        )

    def reply_copies(k):
        peer = lax.rem(me - offset(k) + n, n)
        return (
            copy(reply.at[k], replies.at[me], reply_sent.at[k], reply_got.at[k], peer),
            copy(stat.at[k], stats.at[me], stat_sent.at[k], stat_got.at[k], peer),
        )

    barrier = pltpu.get_barrier_semaphore()

    def greet(k, carry):
        pl.semaphore_signal(
            barrier, inc=1, device_id={"frames": lax.rem(me + k, n)}, device_id_type=MESH
        )
        return carry

    lax.fori_loop(1, n, greet, 0)
    work[...] = anchors[...]
    replies[me] = jnp.zeros(replies.shape[1:], replies.dtype)
    stats[me] = jnp.zeros(stats.shape[1:], stats.dtype)
    pl.semaphore_wait(barrier, n - 1)

    stages = n.bit_length() - 1
    pieces = table.shape[0]

    def ask(k, carry):
        for c in query_copies(k):
            c.start()
        return carry

    base = me * 0
    size = pieces
    bounds = [1 + (n - 1) * i // stages for i in range(stages + 1)]
    later = max(stages - 1, 1)
    asks = [1] + [1 + n // 2 + (n // 2 - 1) * i // later for i in range(stages)]
    for i in range(stages):
        half = size // 2
        bit = (me // 2**i) % 2
        partner = me + 2**i * (1 - 2 * bit)
        mine = base + bit * half
        other = base + (1 - bit) * half
        start = pieces - size
        moving = copy(
            work.at[pl.ds(other, half)],
            arrived.at[pl.ds(start, half)],
            anchor_sent.at[i],
            anchor_got.at[i],
            partner,
        )
        moving.start()
        lax.fori_loop(asks[i], asks[i + 1], ask, 0)
        moving.wait()
        work[pl.ds(mine, half)] = work[pl.ds(mine, half)] + arrived[pl.ds(start, half)]
        base, size = mine, half
    table[pl.ds(base, size)] = work[pl.ds(base, size)]

    masks = head_masks(length)
    rows = GROUP * length
    eye = lax.broadcasted_iota(jnp.int32, (rows, rows), 0) == lax.broadcasted_iota(
        jnp.int32, (rows, rows), 1
    )

    def answer(k, carry):
        source = lax.rem(me - offset(k) + n, n)
        for c in query_copies(k):
            c.wait_recv()
        note = notes_in[source]
        lines = keys_in_all // note.shape[1]
        visible = jnp.concatenate([note[j : j + 1] for j in range(lines)], axis=1) > 0.5
        pieces_out = []
        for g in range(HEADS // GROUP):
            low = g * WIDE
            keys = packed[:, :, inner + low : inner + low + WIDE].reshape(keys_in_all, WIDE)
            values = packed[:, :, 2 * inner + low : 2 * inner + low + WIDE].reshape(
                keys_in_all, WIDE
            )
            out, lse = attend_group(
                queries_in[source, :, low : low + WIDE], keys, values, masks, visible
            )
            reply[k, :, low : low + WIDE] = out.astype(jnp.bfloat16)
            line = jnp.sum(jnp.where(eye, lse, 0.0), axis=0, keepdims=True)
            width = note.shape[1]
            pieces_out += [line[:, j * width : (j + 1) * width] for j in range(rows // width)]
        spare = jnp.zeros((note.shape[0] - len(pieces_out), note.shape[1]), jnp.float32)
        stat[k] = jnp.concatenate(pieces_out + [spare], axis=0)
        for c in reply_copies(k):
            c.start()
        return carry

    for i in reversed(range(stages)):
        bit = (me // 2**i) % 2
        partner = me + 2**i * (1 - 2 * bit)
        moving = copy(
            table.at[pl.ds(base, size)],
            table.at[pl.ds(base, size)],
            anchor_sent.at[stages + i],
            anchor_got.at[stages + i],
            partner,
        )
        moving.start()
        lax.fori_loop(bounds[stages - 1 - i], bounds[stages - i], answer, 0)
        moving.wait()
        base, size = base - bit * size, 2 * size

    def finish(k, carry):
        for c in query_copies(k):
            c.wait_send()
        for c in reply_copies(k):
            c.wait()
        return carry

    lax.fori_loop(1, n, finish, 0)


def attend_own(submap, anchor_ok, packed, table, out_ref, top_ref):
    frames, length, _ = out_ref.shape
    inner = HEADS * HD
    masks = head_masks(length)
    second_half = lax.broadcasted_iota(jnp.int32, (1, 2 * length), 1) >= length
    for i in range(frames):
        f = i
        s = submap[f]
        visible = jnp.where(second_half, anchor_ok[f], 1) > 0
        for g in range(HEADS // GROUP):
            low = g * WIDE
            keys = jnp.concatenate(
                [packed[f, :, inner + low : inner + low + WIDE], table[s, :, 0, :, low : low + WIDE].reshape(length, WIDE)],
                axis=0,
            )
            values = jnp.concatenate(
                [
                    packed[f, :, 2 * inner + low : 2 * inner + low + WIDE],
                    table[s, :, 1, :, low : low + WIDE].reshape(length, WIDE),
                ],
                axis=0,
            )
            out, lse = attend_group(
                packed[f, :, low : low + WIDE], keys, values, masks, visible
            )
            out_ref[i, :, low : low + WIDE] = out
            spread = jnp.where(masks[0], lse[:length], 0.0)
            for h in range(1, GROUP):
                spread = jnp.where(masks[h], lse[h * length : (h + 1) * length], spread)
            top_ref[i, :, low : low + WIDE] = spread


def merge_kernel(
    asker,
    has_peer,
    submap,
    anchor_ok,
    replies,
    stats,
    packed,
    table,
    out_global,
    update,
    acc,
    top,
    total,
):
    frames, length, inner = acc.shape
    attend_own(submap, anchor_ok, packed, table, acc, top)
    total[...] = jnp.ones_like(total)
    rows = GROUP * length
    query_of = lax.broadcasted_iota(jnp.int32, (length, rows), 1) % length
    place = query_of == lax.broadcasted_iota(jnp.int32, (length, rows), 0)
    same_head = (
        lax.broadcasted_iota(jnp.int32, (rows, WIDE), 0) // length
        == lax.broadcasted_iota(jnp.int32, (rows, WIDE), 1) // HD
    )
    spreader = jnp.where(same_head, 1.0, 0.0).astype(jnp.bfloat16)

    def add(b, carry):
        @pl.when(has_peer[b] > 0)
        def _():
            f = asker[b]
            for g in range(HEADS // GROUP):
                cols = slice(g * WIDE, (g + 1) * WIDE)
                lines = stats[b]
                count = rows // lines.shape[1]
                line = jnp.concatenate(
                    [lines[j : j + 1] for j in range(g * count, (g + 1) * count)], axis=1
                )
                notes = split_three(line)
                stacked = jnp.concatenate(
                    [
                        jnp.where(place, part.astype(jnp.float32), 0.0).astype(jnp.bfloat16)
                        for part in notes
                    ],
                    axis=0,
                )
                spread = jnp.dot(stacked, spreader, preferred_element_type=jnp.float32)
                lse = spread[:length] + spread[length : 2 * length] + spread[2 * length :]
                before = top[f, :, cols]
                largest = jnp.maximum(before, lse)
                keep, new = jnp.exp(before - largest), jnp.exp(lse - largest)
                top[f, :, cols] = largest
                total[f, :, cols] = total[f, :, cols] * keep + new
                acc[f, :, cols] = acc[f, :, cols] * keep + (
                    replies[b, :, cols].astype(jnp.float32) * new
                )

        return carry

    lax.fori_loop(0, replies.shape[0], add, 0)
    attended = (acc[...] / total[...]).astype(jnp.bfloat16).reshape(frames * length, inner)
    update[...] = (
        jnp.dot(attended, out_global[...], preferred_element_type=jnp.float32)
        .astype(jnp.bfloat16)
        .reshape(update.shape)
    )


def whole(shape):
    return pl.BlockSpec(shape, lambda *_: (0,) * len(shape))


def local(
    tokens,
    gain_frame,
    qkv_frame,
    out_frame,
    gain_global,
    qkv_global,
    out_global,
    covis,
    submap_ids,
    submap_anchor,
):
    frame_count, token_count, feature_count = tokens.shape
    inner_width = HEADS * HD
    block_count = lax.axis_size("frames")
    position = lax.axis_index("frames")
    submap_count = submap_anchor.shape[0]

    frame_range = jnp.arange(frame_count, dtype=jnp.int32)
    own_ids = position * frame_count + frame_range
    listed_ok = covis >= 0
    owners = jnp.where(listed_ok, covis // frame_count, -1)
    slot_index = covis % frame_count
    peer_ids = jnp.arange(block_count, dtype=jnp.int32)
    touches = owners[:, :, None] == peer_ids[None, None, :]
    asker_index = jnp.max(jnp.where(touches, frame_range[:, None, None], 0), axis=(0, 1))
    lowest = jnp.min(jnp.where(touches, slot_index[:, :, None], frame_count), axis=(0, 1))
    highest = jnp.max(jnp.where(touches, slot_index[:, :, None], -1), axis=(0, 1))
    has_peer = (highest >= 0).astype(jnp.int32)
    request = jnp.stack(
        [
            jnp.where(has_peer > 0, lowest, -1),
            jnp.where((has_peer > 0) & (highest != lowest), highest, -1),
        ],
        axis=1,
    ).reshape(-1)
    submap_range = jnp.arange(submap_count, dtype=jnp.int32)
    anchor_ids = jnp.sum(
        jnp.where(submap_ids[:, None] == submap_range, submap_anchor[None, :], 0), axis=1
    )
    in_list = jnp.any(covis == anchor_ids[:, None], axis=1)
    anchor_ok = ((anchor_ids != own_ids) & jnp.logical_not(in_list)).astype(jnp.int32)
    holding = (submap_anchor // frame_count == position).astype(jnp.int32)
    held = submap_anchor % frame_count

    note_shape = (block_count, 8, 128)
    piece_count = submap_count * token_count // PIECE * 2
    pieces = (piece_count, PIECE, inner_width)
    assert frame_count * token_count <= 1024 and piece_count % block_count == 0
    steps = 2
    each = frame_count // steps
    frame_out, packed, message, notes, anchor_terms = pl.pallas_call(
        front_kernel,
        grid_spec=pltpu.PrefetchScalarGridSpec(
            num_scalar_prefetch=4,
            grid=(steps,),
            in_specs=[
                pl.BlockSpec((each, token_count, feature_count), lambda i, *_: (i, 0, 0)),
                whole((1, feature_count)),
                whole(qkv_frame.shape),
                whole(out_frame.shape),
                whole((1, feature_count)),
                whole(qkv_global.shape),
            ],
            out_specs=[
                pl.BlockSpec((each, token_count, feature_count), lambda i, *_: (i, 0, 0)),
                whole((frame_count, token_count, 3 * inner_width)),
                whole((block_count, token_count, inner_width)),
                whole(note_shape),
                whole(pieces),
            ],
        ),
        out_shape=[
            jax.ShapeDtypeStruct(tokens.shape, jnp.bfloat16),
            jax.ShapeDtypeStruct((frame_count, token_count, 3 * inner_width), jnp.bfloat16),
            jax.ShapeDtypeStruct((block_count, token_count, inner_width), jnp.bfloat16),
            jax.ShapeDtypeStruct(note_shape, jnp.float32),
            jax.ShapeDtypeStruct(pieces, jnp.bfloat16),
        ],
        compiler_params=pltpu.CompilerParams(vmem_limit_bytes=52 * 2**20),
        cost_estimate=pl.CostEstimate(
            flops=4 * 10**9, bytes_accessed=15 * 10**6, transcendentals=10**6
        ),
        name="front",
    )(
        asker_index,
        request,
        holding,
        held,
        tokens,
        gain_frame.reshape(1, -1),
        qkv_frame,
        out_frame,
        gain_global.reshape(1, -1),
        qkv_global,
    )

    stages = block_count.bit_length() - 1
    in_vmem = pl.BlockSpec(memory_space=pltpu.VMEM)
    per_peer = pltpu.SemaphoreType.DMA((block_count,))
    replies, stats, table = pl.pallas_call(
        functools.partial(exchange_kernel, block_count),
        in_specs=[in_vmem] * 4,
        out_specs=[in_vmem] * 3,
        out_shape=[
            jax.ShapeDtypeStruct(message.shape, jnp.bfloat16),
            jax.ShapeDtypeStruct(note_shape, jnp.float32),
            jax.ShapeDtypeStruct(pieces, jnp.bfloat16),
        ],
        scratch_shapes=[
            pltpu.VMEM(message.shape, jnp.bfloat16),
            pltpu.VMEM(note_shape, jnp.float32),
            pltpu.VMEM(message.shape, jnp.bfloat16),
            pltpu.VMEM(note_shape, jnp.float32),
            pltpu.VMEM(pieces, jnp.bfloat16),
            pltpu.VMEM(pieces, jnp.bfloat16),
        ]
        + [per_peer] * 8
        + [pltpu.SemaphoreType.DMA((2 * stages,))] * 2,
        compiler_params=pltpu.CompilerParams(
            collective_id=0, has_side_effects=True, vmem_limit_bytes=44 * 2**20
        ),
        cost_estimate=pl.CostEstimate(
            flops=4 * 10**9, bytes_accessed=8 * 10**6, transcendentals=4 * 10**6
        ),
        name="exchange",
    )(message, notes, packed, anchor_terms)
    table = table.reshape(submap_count, token_count // PIECE, 2, PIECE, inner_width)

    global_update = pl.pallas_call(
        merge_kernel,
        grid_spec=pltpu.PrefetchScalarGridSpec(
            num_scalar_prefetch=4,
            grid=(1,),
            in_specs=[
                whole(replies.shape),
                whole(stats.shape),
                whole(packed.shape),
                whole(table.shape),
                whole(out_global.shape),
            ],
            out_specs=whole(tokens.shape),
            scratch_shapes=[pltpu.VMEM((frame_count, token_count, inner_width), jnp.float32)]
            * 3,
        ),
        out_shape=jax.ShapeDtypeStruct(tokens.shape, jnp.bfloat16),
        compiler_params=pltpu.CompilerParams(vmem_limit_bytes=40 * 2**20),
        cost_estimate=pl.CostEstimate(
            flops=10**9, bytes_accessed=6 * 10**6, transcendentals=10**6
        ),
        name="merge",
    )(asker_index, has_peer, submap_ids, anchor_ok, replies, stats, packed, table, out_global)
    return frame_out, global_update


def solution(mesh):
    return jax.shard_map(
        local,
        mesh=mesh,
        in_specs=(
            P(("parts", "frames"), None, None),
            P(),
            P(),
            P(),
            P(),
            P(),
            P(),
            P(("parts", "frames"), None),
            P(("parts", "frames")),
            P("parts"),
        ),
        out_specs=(P(("parts", "frames"), None, None), P(("parts", "frames"), None, None)),
        check_vma=False,
    )
```

```python
import functools

import jax
import jax.numpy as jnp
from jax import lax
from jax.experimental import pallas as pl
from jax.experimental.pallas import tpu as pltpu
from jax.sharding import PartitionSpec as P

HEADS = 8
HD = 64
CAP_K = 2
GROUP = 4
WIDE = GROUP * HD
PIECE = 16
MESH = pl.DeviceIdType.MESH

masked_score = -1e30


def layer_norm(widened, gain_row):
    centre = jnp.mean(widened, axis=-1, keepdims=True)
    shifted = widened - centre
    variance = jnp.mean(shifted * shifted, axis=-1, keepdims=True)
    return (shifted * lax.rsqrt(variance + 1e-06) * gain_row).astype(jnp.bfloat16)


def head_masks(rows):
    head = lax.broadcasted_iota(jnp.int32, (rows, WIDE), 1) // HD
    return [head == h for h in range(GROUP)]


def attend_group(queries, keys, values, masks, visible=None):
    zero = jnp.zeros_like(queries)
    stacked = jnp.concatenate([jnp.where(m, queries, zero) for m in masks], axis=0)
    scores = lax.dot_general(
        stacked, keys, (((1,), (1,)), ((), ())), preferred_element_type=jnp.float32
    ) * HD ** (-0.5)
    if visible is not None:
        scores = jnp.where(visible, scores, masked_score)
    largest = jnp.max(scores, axis=-1, keepdims=True)
    weights = jnp.exp(scores - largest)
    if visible is not None:
        weights = jnp.where(visible, weights, 0.0)
    totals = jnp.sum(weights, axis=-1, keepdims=True)
    totals = jnp.where(totals > 0.0, totals, 1.0)
    summed = jnp.dot(weights.astype(jnp.bfloat16), values, preferred_element_type=jnp.float32)
    summed = summed * (1.0 / totals)
    rows = queries.shape[0]
    out = jnp.where(masks[0], summed[:rows], 0.0)
    for h in range(1, GROUP):
        out = jnp.where(masks[h], summed[h * rows : (h + 1) * rows], out)
    return out, largest + jnp.log(totals)


def front_kernel(
    asker,
    request,
    holding,
    held,
    tokens,
    gain_frame,
    qkv_frame,
    out_frame,
    gain_global,
    qkv_global,
    frame_out,
    packed,
    message,
    notes,
    anchors,
):
    step = pl.program_id(0)
    frames, length, features = tokens.shape
    inner = HEADS * HD
    rows = frames * length
    x = tokens[...].reshape(rows, features).astype(jnp.float32)
    normed = layer_norm(x, gain_frame[...])
    first = jnp.dot(normed, qkv_frame[...], preferred_element_type=jnp.float32).astype(
        jnp.bfloat16
    )
    masks = head_masks(length)
    attended = []
    for f in range(frames):
        mine = first[f * length : (f + 1) * length]
        parts = []
        for g in range(HEADS // GROUP):
            low = g * WIDE
            out, _ = attend_group(
                mine[:, low : low + WIDE],
                mine[:, inner + low : inner + low + WIDE],
                mine[:, 2 * inner + low : 2 * inner + low + WIDE],
                masks,
            )
            parts.append(out.astype(jnp.bfloat16))
        attended.append(jnp.concatenate(parts, axis=1))
    attended = jnp.concatenate(attended, axis=0)
    after = (
        x + jnp.dot(attended, out_frame[...], preferred_element_type=jnp.float32)
    ).astype(jnp.bfloat16)
    frame_out[...] = after.reshape(frames, length, features)
    normed = layer_norm(after.astype(jnp.float32), gain_global[...])
    second = jnp.dot(normed, qkv_global[...], preferred_element_type=jnp.float32).astype(
        jnp.bfloat16
    )
    packed[pl.ds(step * frames, frames)] = second.reshape(frames, length, 3 * inner)

    @pl.when(step == pl.num_programs(0) - 1)
    def _():
        row = lax.broadcasted_iota(jnp.int32, notes.shape[1:], 0)
        lane = lax.broadcasted_iota(jnp.int32, notes.shape[1:], 1)
        frame_of_key = (row * lane.shape[1] + lane) // length

        def put(b, carry):
            message[b] = packed[asker[b], :, :inner]
            wanted = (frame_of_key == request[2 * b]) | (frame_of_key == request[2 * b + 1])
            notes[b] = jnp.where(wanted, 1.0, 0.0)
            return carry

        lax.fori_loop(0, message.shape[0], put, 0)
        count = length // PIECE

        def hold(s, carry):
            taken = packed[held[s], :, inner:]
            taken = jnp.where(holding[s] > 0, taken, jnp.zeros_like(taken))
            for r in range(count):
                for c in range(2):
                    anchors[(s * count + r) * 2 + c] = taken[
                        r * PIECE : (r + 1) * PIECE, c * inner : (c + 1) * inner
                    ]
            return carry

        lax.fori_loop(0, held.shape[0], hold, 0)


def split_three(values):
    high = values.astype(jnp.bfloat16)
    rest = values - high.astype(jnp.float32)
    middle = rest.astype(jnp.bfloat16)
    low = (rest - middle.astype(jnp.float32)).astype(jnp.bfloat16)
    return high, middle, low


def exchange_kernel(
    n,
    queries,
    notes,
    packed,
    anchors,
    replies,
    stats,
    table,
    queries_in,
    notes_in,
    reply,
    stat,
    arrived,
    work,
    query_sent,
    query_got,
    note_sent,
    note_got,
    reply_sent,
    reply_got,
    stat_sent,
    stat_got,
    anchor_sent,
    anchor_got,
):
    me = lax.axis_index("frames")
    frames, length, _ = packed.shape
    inner = HEADS * HD
    keys_in_all = frames * length

    def copy(source, target, sent, got, device):
        return pltpu.make_async_remote_copy(
            src_ref=source,
            dst_ref=target,
            send_sem=sent,
            recv_sem=got,
            device_id={"frames": device},
            device_id_type=MESH,
        )

    def offset(j):
        odd = (j - 1) % 2
        return n // 2 + (1 - odd) * ((j - 1) // 2) - odd * (j // 2)

    def query_copies(k):
        peer = lax.rem(me + offset(k), n)
        return (
            copy(queries.at[peer], queries_in.at[me], query_sent.at[k], query_got.at[k], peer),
            copy(notes.at[peer], notes_in.at[me], note_sent.at[k], note_got.at[k], peer),
        )

    def reply_copies(k):
        peer = lax.rem(me - offset(k) + n, n)
        return (
            copy(reply.at[k], replies.at[me], reply_sent.at[k], reply_got.at[k], peer),
            copy(stat.at[k], stats.at[me], stat_sent.at[k], stat_got.at[k], peer),
        )

    barrier = pltpu.get_barrier_semaphore()

    def greet(k, carry):
        pl.semaphore_signal(
            barrier, inc=1, device_id={"frames": lax.rem(me + k, n)}, device_id_type=MESH
        )
        return carry

    lax.fori_loop(1, n, greet, 0)
    work[...] = anchors[...]
    replies[me] = jnp.zeros(replies.shape[1:], replies.dtype)
    stats[me] = jnp.zeros(stats.shape[1:], stats.dtype)
    pl.semaphore_wait(barrier, n - 1)

    stages = n.bit_length() - 1
    pieces = table.shape[0]

    def ask(k, carry):
        for c in query_copies(k):
            c.start()
        return carry

    base = me * 0
    size = pieces
    bounds = [1 + (n - 1) * i // stages for i in range(stages + 1)]
    asks = [1] + [n - (n >> (i + 2)) for i in range(stages)]
    for i in range(stages):
        half = size // 2
        bit = (me // 2**i) % 2
        partner = me + 2**i * (1 - 2 * bit)
        mine = base + bit * half
        other = base + (1 - bit) * half
        start = pieces - size
        moving = copy(
            work.at[pl.ds(other, half)],
            arrived.at[pl.ds(start, half)],
            anchor_sent.at[i],
            anchor_got.at[i],
            partner,
        )
        moving.start()
        lax.fori_loop(asks[i], asks[i + 1], ask, 0)
        moving.wait()
        work[pl.ds(mine, half)] = work[pl.ds(mine, half)] + arrived[pl.ds(start, half)]
        base, size = mine, half
    table[pl.ds(base, size)] = work[pl.ds(base, size)]

    masks = head_masks(length)
    rows = GROUP * length
    eye = lax.broadcasted_iota(jnp.int32, (rows, rows), 0) == lax.broadcasted_iota(
        jnp.int32, (rows, rows), 1
    )

    def answer(k, carry):
        source = lax.rem(me - offset(k) + n, n)
        for c in query_copies(k):
            c.wait_recv()
        note = notes_in[source]
        lines = keys_in_all // note.shape[1]
        visible = jnp.concatenate([note[j : j + 1] for j in range(lines)], axis=1) > 0.5
        pieces_out = []
        for g in range(HEADS // GROUP):
            low = g * WIDE
            keys = packed[:, :, inner + low : inner + low + WIDE].reshape(keys_in_all, WIDE)
            values = packed[:, :, 2 * inner + low : 2 * inner + low + WIDE].reshape(
                keys_in_all, WIDE
            )
            out, lse = attend_group(
                queries_in[source, :, low : low + WIDE], keys, values, masks, visible
            )
            reply[k, :, low : low + WIDE] = out.astype(jnp.bfloat16)
            line = jnp.sum(jnp.where(eye, lse, 0.0), axis=0, keepdims=True)
            width = note.shape[1]
            pieces_out += [line[:, j * width : (j + 1) * width] for j in range(rows // width)]
        spare = jnp.zeros((note.shape[0] - len(pieces_out), note.shape[1]), jnp.float32)
        stat[k] = jnp.concatenate(pieces_out + [spare], axis=0)
        for c in reply_copies(k):
            c.start()
        return carry

    for i in reversed(range(stages)):
        bit = (me // 2**i) % 2
        partner = me + 2**i * (1 - 2 * bit)
        moving = copy(
            table.at[pl.ds(base, size)],
            table.at[pl.ds(base, size)],
            anchor_sent.at[stages + i],
            anchor_got.at[stages + i],
            partner,
        )
        moving.start()
        lax.fori_loop(bounds[stages - 1 - i], bounds[stages - i], answer, 0)
        moving.wait()
        base, size = base - bit * size, 2 * size

    def finish(k, carry):
        for c in query_copies(k):
            c.wait_send()
        for c in reply_copies(k):
            c.wait()
        return carry

    lax.fori_loop(1, n, finish, 0)


def attend_own(submap, anchor_ok, packed, table, out_ref, top_ref):
    frames, length, _ = out_ref.shape
    inner = HEADS * HD
    masks = head_masks(length)
    second_half = lax.broadcasted_iota(jnp.int32, (1, 2 * length), 1) >= length
    for i in range(frames):
        f = i
        s = submap[f]
        visible = jnp.where(second_half, anchor_ok[f], 1) > 0
        for g in range(HEADS // GROUP):
            low = g * WIDE
            keys = jnp.concatenate(
                [packed[f, :, inner + low : inner + low + WIDE], table[s, :, 0, :, low : low + WIDE].reshape(length, WIDE)],
                axis=0,
            )
            values = jnp.concatenate(
                [
                    packed[f, :, 2 * inner + low : 2 * inner + low + WIDE],
                    table[s, :, 1, :, low : low + WIDE].reshape(length, WIDE),
                ],
                axis=0,
            )
            out, lse = attend_group(
                packed[f, :, low : low + WIDE], keys, values, masks, visible
            )
            out_ref[i, :, low : low + WIDE] = out
            spread = jnp.where(masks[0], lse[:length], 0.0)
            for h in range(1, GROUP):
                spread = jnp.where(masks[h], lse[h * length : (h + 1) * length], spread)
            top_ref[i, :, low : low + WIDE] = spread


def merge_kernel(
    asker,
    has_peer,
    submap,
    anchor_ok,
    replies,
    stats,
    packed,
    table,
    out_global,
    update,
    acc,
    top,
    total,
):
    frames, length, inner = acc.shape
    attend_own(submap, anchor_ok, packed, table, acc, top)
    total[...] = jnp.ones_like(total)
    rows = GROUP * length
    query_of = lax.broadcasted_iota(jnp.int32, (length, rows), 1) % length
    place = query_of == lax.broadcasted_iota(jnp.int32, (length, rows), 0)
    same_head = (
        lax.broadcasted_iota(jnp.int32, (rows, WIDE), 0) // length
        == lax.broadcasted_iota(jnp.int32, (rows, WIDE), 1) // HD
    )
    spreader = jnp.where(same_head, 1.0, 0.0).astype(jnp.bfloat16)

    def add(b, carry):
        @pl.when(has_peer[b] > 0)
        def _():
            f = asker[b]
            for g in range(HEADS // GROUP):
                cols = slice(g * WIDE, (g + 1) * WIDE)
                lines = stats[b]
                count = rows // lines.shape[1]
                line = jnp.concatenate(
                    [lines[j : j + 1] for j in range(g * count, (g + 1) * count)], axis=1
                )
                notes = split_three(line)
                stacked = jnp.concatenate(
                    [
                        jnp.where(place, part.astype(jnp.float32), 0.0).astype(jnp.bfloat16)
                        for part in notes
                    ],
                    axis=0,
                )
                spread = jnp.dot(stacked, spreader, preferred_element_type=jnp.float32)
                lse = spread[:length] + spread[length : 2 * length] + spread[2 * length :]
                before = top[f, :, cols]
                largest = jnp.maximum(before, lse)
                keep, new = jnp.exp(before - largest), jnp.exp(lse - largest)
                top[f, :, cols] = largest
                total[f, :, cols] = total[f, :, cols] * keep + new
                acc[f, :, cols] = acc[f, :, cols] * keep + (
                    replies[b, :, cols].astype(jnp.float32) * new
                )

        return carry

    lax.fori_loop(0, replies.shape[0], add, 0)
    attended = (acc[...] / total[...]).astype(jnp.bfloat16).reshape(frames * length, inner)
    update[...] = (
        jnp.dot(attended, out_global[...], preferred_element_type=jnp.float32)
        .astype(jnp.bfloat16)
        .reshape(update.shape)
    )


def whole(shape):
    return pl.BlockSpec(shape, lambda *_: (0,) * len(shape))


def local(
    tokens,
    gain_frame,
    qkv_frame,
    out_frame,
    gain_global,
    qkv_global,
    out_global,
    covis,
    submap_ids,
    submap_anchor,
):
    frame_count, token_count, feature_count = tokens.shape
    inner_width = HEADS * HD
    block_count = lax.axis_size("frames")
    position = lax.axis_index("frames")
    submap_count = submap_anchor.shape[0]

    frame_range = jnp.arange(frame_count, dtype=jnp.int32)
    own_ids = position * frame_count + frame_range
    listed_ok = covis >= 0
    owners = jnp.where(listed_ok, covis // frame_count, -1)
    slot_index = covis % frame_count
    peer_ids = jnp.arange(block_count, dtype=jnp.int32)
    touches = owners[:, :, None] == peer_ids[None, None, :]
    asker_index = jnp.max(jnp.where(touches, frame_range[:, None, None], 0), axis=(0, 1))
    lowest = jnp.min(jnp.where(touches, slot_index[:, :, None], frame_count), axis=(0, 1))
    highest = jnp.max(jnp.where(touches, slot_index[:, :, None], -1), axis=(0, 1))
    has_peer = (highest >= 0).astype(jnp.int32)
    request = jnp.stack(
        [
            jnp.where(has_peer > 0, lowest, -1),
            jnp.where((has_peer > 0) & (highest != lowest), highest, -1),
        ],
        axis=1,
    ).reshape(-1)
    submap_range = jnp.arange(submap_count, dtype=jnp.int32)
    anchor_ids = jnp.sum(
        jnp.where(submap_ids[:, None] == submap_range, submap_anchor[None, :], 0), axis=1
    )
    in_list = jnp.any(covis == anchor_ids[:, None], axis=1)
    anchor_ok = ((anchor_ids != own_ids) & jnp.logical_not(in_list)).astype(jnp.int32)
    holding = (submap_anchor // frame_count == position).astype(jnp.int32)
    held = submap_anchor % frame_count

    note_shape = (block_count, 8, 128)
    piece_count = submap_count * token_count // PIECE * 2
    pieces = (piece_count, PIECE, inner_width)
    assert frame_count * token_count <= 1024 and piece_count % block_count == 0
    steps = 2
    each = frame_count // steps
    frame_out, packed, message, notes, anchor_terms = pl.pallas_call(
        front_kernel,
        grid_spec=pltpu.PrefetchScalarGridSpec(
            num_scalar_prefetch=4,
            grid=(steps,),
            in_specs=[
                pl.BlockSpec((each, token_count, feature_count), lambda i, *_: (i, 0, 0)),
                whole((1, feature_count)),
                whole(qkv_frame.shape),
                whole(out_frame.shape),
                whole((1, feature_count)),
                whole(qkv_global.shape),
            ],
            out_specs=[
                pl.BlockSpec((each, token_count, feature_count), lambda i, *_: (i, 0, 0)),
                whole((frame_count, token_count, 3 * inner_width)),
                whole((block_count, token_count, inner_width)),
                whole(note_shape),
                whole(pieces),
            ],
        ),
        out_shape=[
            jax.ShapeDtypeStruct(tokens.shape, jnp.bfloat16),
            jax.ShapeDtypeStruct((frame_count, token_count, 3 * inner_width), jnp.bfloat16),
            jax.ShapeDtypeStruct((block_count, token_count, inner_width), jnp.bfloat16),
            jax.ShapeDtypeStruct(note_shape, jnp.float32),
            jax.ShapeDtypeStruct(pieces, jnp.bfloat16),
        ],
        compiler_params=pltpu.CompilerParams(vmem_limit_bytes=52 * 2**20),
        cost_estimate=pl.CostEstimate(
            flops=4 * 10**9, bytes_accessed=15 * 10**6, transcendentals=10**6
        ),
        name="front",
    )(
        asker_index,
        request,
        holding,
        held,
        tokens,
        gain_frame.reshape(1, -1),
        qkv_frame,
        out_frame,
        gain_global.reshape(1, -1),
        qkv_global,
    )

    stages = block_count.bit_length() - 1
    in_vmem = pl.BlockSpec(memory_space=pltpu.VMEM)
    per_peer = pltpu.SemaphoreType.DMA((block_count,))
    replies, stats, table = pl.pallas_call(
        functools.partial(exchange_kernel, block_count),
        in_specs=[in_vmem] * 4,
        out_specs=[in_vmem] * 3,
        out_shape=[
            jax.ShapeDtypeStruct(message.shape, jnp.bfloat16),
            jax.ShapeDtypeStruct(note_shape, jnp.float32),
            jax.ShapeDtypeStruct(pieces, jnp.bfloat16),
        ],
        scratch_shapes=[
            pltpu.VMEM(message.shape, jnp.bfloat16),
            pltpu.VMEM(note_shape, jnp.float32),
            pltpu.VMEM(message.shape, jnp.bfloat16),
            pltpu.VMEM(note_shape, jnp.float32),
            pltpu.VMEM(pieces, jnp.bfloat16),
            pltpu.VMEM(pieces, jnp.bfloat16),
        ]
        + [per_peer] * 8
        + [pltpu.SemaphoreType.DMA((2 * stages,))] * 2,
        compiler_params=pltpu.CompilerParams(
            collective_id=0, has_side_effects=True, vmem_limit_bytes=44 * 2**20
        ),
        cost_estimate=pl.CostEstimate(
            flops=4 * 10**9, bytes_accessed=8 * 10**6, transcendentals=4 * 10**6
        ),
        name="exchange",
    )(message, notes, packed, anchor_terms)
    table = table.reshape(submap_count, token_count // PIECE, 2, PIECE, inner_width)

    global_update = pl.pallas_call(
        merge_kernel,
        grid_spec=pltpu.PrefetchScalarGridSpec(
            num_scalar_prefetch=4,
            grid=(1,),
            in_specs=[
                whole(replies.shape),
                whole(stats.shape),
                whole(packed.shape),
                whole(table.shape),
                whole(out_global.shape),
            ],
            out_specs=whole(tokens.shape),
            scratch_shapes=[pltpu.VMEM((frame_count, token_count, inner_width), jnp.float32)]
            * 3,
        ),
        out_shape=jax.ShapeDtypeStruct(tokens.shape, jnp.bfloat16),
        compiler_params=pltpu.CompilerParams(vmem_limit_bytes=40 * 2**20),
        cost_estimate=pl.CostEstimate(
            flops=10**9, bytes_accessed=6 * 10**6, transcendentals=10**6
        ),
        name="merge",
    )(asker_index, has_peer, submap_ids, anchor_ok, replies, stats, packed, table, out_global)
    return frame_out, global_update


def solution(mesh):
    return jax.shard_map(
        local,
        mesh=mesh,
        in_specs=(
            P(("parts", "frames"), None, None),
            P(),
            P(),
            P(),
            P(),
            P(),
            P(),
            P(("parts", "frames"), None),
            P(("parts", "frames")),
            P("parts"),
        ),
        out_specs=(P(("parts", "frames"), None, None), P(("parts", "frames"), None, None)),
        check_vma=False,
    )
```
